32 devices in a mesh: row: 4 (over y, x), col: 8 (over z, core).
Axes of the slice: x: 2, y: 2, z: 4, core: 2. Of those that a mesh axis runs over, the one named last changes fastest.
Arguments:
- covariance: float32 [4096, 4096], P('row', 'col'), may hold values from -7 to 14, as said below
- wind_mask: int32 [2, 4096], replicated, may hold values 0 or 1
- wind_speed: float32 [2, 4096], replicated, may hold values from 0.02 to 0.3
- obs_cells: int32 [256, 128], replicated, may hold values from 0 to 4095
- obs_scale: float32 [256], replicated, may hold values from 0.05 to 0.2
- gain: bfloat16 [4096, 256], P('row'), may hold values from -0.375 to 0.375
Outputs:
- updated: float32 [4096, 4096], P('row', 'col')
The draws below stay inside these ranges and needn't reach their ends.
Inputs may be any that keep to these rules, and one draw needn't show every extreme that they name: A covariance window.
All inputs are finite; a program needn't handle non-finite values.
Results may differ from the reference program's by a relative error of at most 0.0003.
Values sent between devices are 32-bit elements; how exact they have to be, the bound alone decides.
A program may use at most 64 MiB of HBM per device.

```python
import jax
import jax.numpy as jnp
from jax import lax

MAPX = 256
NOBS = 256
FOOT = 128
W = 4096


def draw_covariance(key, part):
    first_key = jax.random.fold_in(jax.random.fold_in(key, 17), 0)
    matrix = jnp.clip(jax.random.normal(first_key, (W, W), jnp.float32), -4.0, 4.0) * 0.5
    matrix = matrix + 2.0 * jnp.eye(W, dtype=jnp.float32)
    return matrix.astype(jnp.float32)


def plant(array, rng, smallest, largest):
    longest = array.shape.index(max(array.shape))
    spots = []
    for shift in (0, 1):
        where = [jax.random.randint(jax.random.fold_in(rng, axis), (), 0, length) for axis, length in enumerate(array.shape)]
        where[longest] = (where[longest] + shift) % array.shape[longest]
        spots.append(tuple(where))
    return array.at[spots[0]].set(smallest).at[spots[1]].set(largest)


def levels(rng, dims, shards, low, high):
    level = 1.0
    for position, parts in shards:
        steps = jax.random.uniform(jax.random.fold_in(jax.random.fold_in(rng, 6), position), (parts,), jnp.float32, low / len(shards), high / len(shards))
        level = level * jnp.repeat(jnp.exp(steps), dims[position] // parts).reshape((-1,) + (1,) * (len(dims) - 1 - position))
    return level


def normal_values(key, extent, deviation, most, cuts=(), kind=jnp.bfloat16):
    values = jax.random.normal(key, extent, jnp.float32) * deviation
    if len(cuts) > 0:
        values = levels(key, extent, cuts, -0.22, 0.18) * values
    return jnp.clip(values, min=-most, max=most).astype(kind)


def setup_inputs(seed: int = 0) -> dict:
    streams_of = jax.random.split(jax.random.key(seed), 7)
    covariance = draw_covariance(jax.random.fold_in(streams_of[6], 71), 0)
    wind_mask = plant((jax.random.randint(streams_of[1], (2, W), 0, 2) < 1).astype(jnp.int32), jax.random.fold_in(streams_of[1], 1), 0, 1)
    wind_speed = jnp.clip(jax.random.uniform(streams_of[2], (2, W), jnp.float32, 0.02, 0.3), 0.02, 0.3)
    obs_cells = plant(jax.random.randint(streams_of[3], (NOBS, FOOT), 0, W), jax.random.fold_in(streams_of[3], 1), 0, W - 1).astype(jnp.int32)
    obs_scale = jnp.clip(jax.random.uniform(streams_of[4], (NOBS,), jnp.float32, 0.05, 0.2), 0.05, 0.2)
    gain = normal_values(streams_of[5], (W, NOBS), NOBS ** -0.5, 0.375, ((0, 4),))
    return {"covariance": covariance, "wind_mask": wind_mask, "wind_speed": wind_speed, "obs_cells": obs_cells, "obs_scale": obs_scale, "gain": gain}


diffusion = 0.05


def coefficients(wind_mask, wind_speed):
    cell_total = wind_speed.shape[1]
    cells = jnp.arange(cell_total, dtype=jnp.int32)
    map_column = cells % MAPX
    map_row = cells // MAPX
    last_row = cell_total // MAPX - 1
    speed_x = wind_speed[0]
    speed_y = wind_speed[1]
    sign_x = wind_mask[0].astype(jnp.float32)
    sign_y = wind_mask[1].astype(jnp.float32)
    middle = 1.0 - speed_x - speed_y - 4.0 * diffusion
    western = jnp.where(map_column > 0, speed_x * sign_x + diffusion, 0.0)
    eastern = jnp.where(map_column < MAPX - 1, speed_x * (1.0 - sign_x) + diffusion, 0.0)
    northern = jnp.where(map_row > 0, speed_y * sign_y + diffusion, 0.0)
    southern = jnp.where(map_row < last_row, speed_y * (1.0 - sign_y) + diffusion, 0.0)
    return jnp.stack([middle, western, eastern, northern, southern]).astype(jnp.float32)


def transport(extended, coef, along_dim):
    length = extended.shape[along_dim] - 2 * MAPX
    if along_dim == 0:
        weights = coef[:, :, None]
    else:
        weights = coef[:, None, :]

    def window_at(offset):
        return lax.slice_in_dim(extended, offset, offset + length, axis=along_dim)

    result = weights[0] * window_at(MAPX) + weights[1] * window_at(MAPX - 1)
    result = result + weights[2] * window_at(MAPX + 1)
    result = result + weights[3] * window_at(0) + weights[4] * window_at(2 * MAPX)
    return result


def reference(covariance, wind_mask, wind_speed, obs_cells, obs_scale, gain):
    table = coefficients(wind_mask, wind_speed)
    moved_field = covariance
    for repeat in range(2):
        moved_field = transport(jnp.pad(moved_field, ((MAPX, MAPX), (0, 0))), table, 0)
        moved_field = transport(jnp.pad(moved_field, ((0, 0), (MAPX, MAPX))), table, 1)

    def observe(inputs):
        cell_list, weight_one = inputs
        return weight_one * jnp.sum(moved_field[cell_list], axis=0)

    observed = lax.map(observe, (obs_cells, obs_scale))
    update = jnp.dot(gain.astype(jnp.float32), observed, precision=lax.Precision.HIGHEST, preferred_element_type=jnp.float32)
    return moved_field - update
```

```python
import functools

import jax
import jax.numpy as jnp
from jax import lax
from jax.experimental import pallas as pl
from jax.experimental.pallas import tpu as pltpu
from jax.sharding import PartitionSpec as P

MAPX = 256
LANES = 128
CHUNK = 128
TILE = 16
diffusion = 0.05
MESH = pl.DeviceIdType.MESH


def split(x):
    high = x.astype(jnp.bfloat16)
    return high, (x - high.astype(jnp.float32)).astype(jnp.bfloat16)


def dot(a, b):
    return jnp.dot(a, b, preferred_element_type=jnp.float32)


def coef_block(mask_ref, speed_ref, g, map_rows):
    inside = jnp.logical_and(g >= 0, g < map_rows)
    start = pl.multiple_of(jnp.clip(g, 0, map_rows - 1) * MAPX, MAPX)
    where = pl.ds(start, MAPX)
    speed_x = speed_ref[0:1, where]
    speed_y = speed_ref[1:2, where]
    sign_x = mask_ref[0:1, where].astype(jnp.float32)
    sign_y = mask_ref[1:2, where].astype(jnp.float32)
    column = lax.broadcasted_iota(jnp.int32, (1, MAPX), 1)
    valid = jnp.where(inside, 1.0, 0.0)
    north = jnp.where(g > 0, valid, 0.0)
    south = jnp.where(g < map_rows - 1, valid, 0.0)
    return (
        (1.0 - speed_x - speed_y - 4.0 * diffusion) * valid,
        jnp.where(column > 0, speed_x * sign_x + diffusion, 0.0) * valid,
        jnp.where(column < MAPX - 1, speed_x * (1.0 - sign_x) + diffusion, 0.0) * valid,
        (speed_y * sign_y + diffusion) * north,
        (speed_y * (1.0 - sign_y) + diffusion) * south,
    )


def kernel(
    nr, nc, cov, mask_ref, speed_ref, cells_ref, scale_ref,
    moved_ref, obs_out,
    own, lh, rh, V, Y, ccol, crow, rc, sbuf, s2, tbuf, ah, al, part, rsbuf, obs,
    own_sem, zs, zr, hs, hr, rs_s, rs_r, ag_s, ag_r,
):
    rows, cols = cov.shape
    n_obs = cells_ref.shape[0]
    map_rows = speed_ref.shape[1] // MAPX
    H = 2 * MAPX
    rb, cb = rows // MAPX, cols // MAPX
    nchunk = rows // CHUNK
    half = nchunk // 2
    me_r, me_c = lax.axis_index("row"), lax.axis_index("col")
    has_up, has_down = me_r > 0, me_r < nr - 1
    has_left, has_right = me_c > 0, me_c < nc - 1
    up, down, left, right = me_r - 1, me_r + 1, me_c - 1, me_c + 1
    bits = []
    b = nr // 2
    while b:
        bits.append(b)
        b //= 2

    barrier = pltpu.get_barrier_semaphore()
    for flag, dev in ((has_up, (up, me_c)), (has_down, (down, me_c)), (has_left, (me_r, left)), (has_right, (me_r, right))):
        @pl.when(flag)
        def _(dev=dev):
            pl.semaphore_signal(barrier, inc=1, device_id=dev, device_id_type=MESH)
    partners = []
    for b in bits:
        upper = lax.rem(me_r // b, 2)
        partner = me_r + b - 2 * b * upper
        partners.append((upper, partner))
        if b > 1:
            pl.semaphore_signal(barrier, inc=1, device_id=(partner, me_c), device_id_type=MESH)
    own_copy = pltpu.make_async_copy(cov, own, own_sem)
    own_copy.start()
    peers = len(bits) - 1
    for flag in (has_up, has_down, has_left, has_right):
        peers = peers + flag.astype(jnp.int32)
    pl.semaphore_wait(barrier, peers)

    def chunk_base(d, lower):
        if lower:
            q = half // 2
            index = half + q + d - half * (d // q)
        else:
            index = d
        return pl.multiple_of(index * CHUNK, CHUNK)

    def zcopy(d, lower, side):
        base = chunk_base(d, lower)
        slot = d * 2 + lower
        dst = (rh, lh)[side]
        return pltpu.make_async_remote_copy(
            src_ref=cov.at[pl.ds(base, CHUNK), :], dst_ref=dst.at[pl.ds(base, CHUNK), :],
            send_sem=zs.at[side, slot], recv_sem=zr.at[side, slot],
            device_id=(me_r, (left, right)[side]), device_id_type=MESH)

    def hcopy(d, lower):
        base = chunk_base(d, lower)
        dst = base - H if lower else base + H + rows
        return pltpu.make_async_remote_copy(
            src_ref=V.at[:, pl.ds(H + base, CHUNK), :],
            dst_ref=V.at[:, pl.ds(pl.multiple_of(dst, CHUNK), CHUNK), :],
            send_sem=hs.at[lower, d], recv_sem=hr.at[lower, d],
            device_id=(down if lower else up, me_c), device_id_type=MESH)

    def zstart(d, _):
        for lower in (0, 1):
            @pl.when(has_left)
            def _():
                zcopy(d, lower, 0).start()

            @pl.when(has_right)
            def _():
                zcopy(d, lower, 1).start()
        return 0

    lax.fori_loop(0, half, zstart, 0)

    @pl.when(jnp.logical_not(has_left))
    def _():
        lh[...] = jnp.zeros_like(lh)

    @pl.when(jnp.logical_not(has_right))
    def _():
        rh[...] = jnp.zeros_like(rh)

    @pl.when(jnp.logical_not(has_up))
    def _():
        V[:, 0:H, :] = jnp.zeros((V.shape[0], H, LANES), jnp.float32)

    @pl.when(jnp.logical_not(has_down))
    def _():
        V[:, H + rows:, :] = jnp.zeros((V.shape[0], H, LANES), jnp.float32)

    for b in range(cb + 4):
        for k, v in enumerate(coef_block(mask_ref, speed_ref, me_c * cb + b - 2, map_rows)):
            ccol[b, k:k + 1, :] = v
    for b in range(rb + 4):
        for k, v in enumerate(coef_block(mask_ref, speed_ref, me_r * rb + b - 2, map_rows)):
            crow[b, k:k + 1, :] = v

    own_copy.wait()

    def col_step(v, first, count):
        out = []
        for i in range(count):
            c = [ccol[first + i, k:k + 1, :] for k in range(5)]
            x = v[i + 1]
            r = c[0] * x + c[1] * pltpu.roll(x, 1, 1)
            r = r + c[2] * pltpu.roll(x, MAPX - 1, 1)
            out.append(r + c[3] * v[i] + c[4] * v[i + 2])
        return out

    def col_chunk(base):
        def body(t, _):
            at = pl.ds(pl.multiple_of(base + t * TILE, TILE), TILE)
            v = [lh[at, cols - H + j * MAPX:cols - H + (j + 1) * MAPX] for j in range(2)]
            v += [own[at, j * MAPX:(j + 1) * MAPX] for j in range(cb)]
            v += [rh[at, j * MAPX:(j + 1) * MAPX] for j in range(2)]
            y = col_step(v, 1, cb + 2)
            z = col_step(y, 2, cb)
            put = pl.ds(pl.multiple_of(H + base + t * TILE, TILE), TILE)
            for j in range(cb):
                for l in range(2):
                    V[2 * j + l, put, :] = z[j][:, l * LANES:(l + 1) * LANES]
            return 0
        lax.fori_loop(0, CHUNK // TILE, body, 0)

    wide = rows + 2 * H
    nh = wide // LANES
    origin = me_r * rows - H
    lo_iota = lax.broadcasted_iota(jnp.int32, (LANES, LANES), 0)
    hi_iota = lax.broadcasted_iota(jnp.int32, (nh, LANES), 0)

    def count_group(g, _):
        base = pl.multiple_of(g * 8, 8)
        idx = cells_ref[pl.ds(base, 8), :] - origin
        hi = lax.shift_right_arithmetic(idx, 7)
        lo = jnp.bitwise_and(idx, LANES - 1)
        for i in range(8):
            one_hi = jnp.where(hi[i:i + 1, :] == hi_iota, 1.0, 0.0).astype(jnp.bfloat16)
            one_lo = jnp.where(lo[i:i + 1, :] == lo_iota, 1.0, 0.0).astype(jnp.bfloat16)
            counts = lax.dot_general(one_hi, one_lo, (((1,), (1,)), ((), ())), preferred_element_type=jnp.float32)
            sbuf[pl.ds(pl.multiple_of((base + i) * nh, 8), nh), :] = counts * scale_ref[base + i]
        return 0

    nrc = (rows + H) // LANES
    groups = n_obs // 8
    for d in range(half):
        for lower in (0, 1):
            @pl.when(has_left)
            def _():
                zcopy(d, lower, 0).wait_send()
                zcopy(d, lower, 1).wait_recv()

            @pl.when(has_right)
            def _():
                zcopy(d, lower, 1).wait_send()
                zcopy(d, lower, 0).wait_recv()
            col_chunk(chunk_base(d, lower))

            @pl.when(has_down if lower else has_up)
            def _():
                hcopy(d, lower).start()
        if d < half - 1:
            g0 = groups * d // (half - 1)
            g1 = groups * (d + 1) // (half - 1)
            lax.fori_loop(g0, g1, count_group, 0)
        if d == half - 2:
            for h in range(nh):
                s2[h // 2, :, (h % 2) * LANES:(h % 2 + 1) * LANES] = sbuf[pl.ds(h, n_obs, stride=nh), :]

            def adjoint(src, at, b, offset):
                def get(i):
                    return src[i - offset, at, :]
                c = [crow[b, k:k + 1, :] for k in range(3)]
                x = get(b)
                r = c[0] * x + pltpu.roll(c[1] * x, MAPX - 1, 1) + pltpu.roll(c[2] * x, 1, 1)
                return r + crow[b + 1, 3:4, :] * get(b + 1) + crow[b - 1, 4:5, :] * get(b - 1)

            def step_one(t, _):
                at = pl.ds(pl.multiple_of(t * TILE, TILE), TILE)
                for b in range(1, rb + 3):
                    tbuf[b - 1, at, :] = adjoint(s2, at, b, 0)
                return 0

            def step_two(t, _):
                at = pl.ds(pl.multiple_of(t * TILE, TILE), TILE)
                for b in range(2, rb + 2):
                    a_hi, a_lo = split(adjoint(tbuf, at, b, 1))
                    ah[b - 2, at, :] = a_hi
                    al[b - 2, at, :] = a_lo
                return 0

            lax.fori_loop(0, n_obs // TILE, step_one, 0)
            lax.fori_loop(0, n_obs // TILE, step_two, 0)
            for b in (0, rb - 1):
                observe_block(V, ah, al, part, b, b == 0, H, cols)
    for b in range(1, rb - 1):
        observe_block(V, ah, al, part, b, False, H, cols)

    def rs_copy(s):
        upper, partner = partners[s]
        size = n_obs >> (s + 1)
        src = offs[s] + (1 - upper) * size
        return pltpu.make_async_remote_copy(
            src_ref=part.at[pl.ds(pl.multiple_of(src, 8), size), :],
            dst_ref=rsbuf.at[pl.ds(n_obs - 2 * size, size), :],
            send_sem=rs_s.at[s], recv_sem=rs_r.at[s], device_id=(partner, me_c), device_id_type=MESH)

    offs = [jnp.int32(0)]
    for s in range(len(bits)):
        offs.append(offs[s] + partners[s][0] * (n_obs >> (s + 1)))

    def rs_finish(s):
        size = n_obs >> (s + 1)
        copy = rs_copy(s)
        copy.wait()
        at = pl.ds(pl.multiple_of(offs[s + 1], 8), size)
        part[at, :] = part[at, :] + rsbuf[n_obs - 2 * size:n_obs - size, :]

    def ag_copy(s):
        size = n_obs >> (s + 1)
        at = pl.ds(pl.multiple_of(offs[s + 1], 8), size)
        return pltpu.make_async_remote_copy(
            src_ref=obs.at[at, :], dst_ref=obs.at[at, :],
            send_sem=ag_s.at[s], recv_sem=ag_r.at[s], device_id=(partners[s][1], me_c), device_id_type=MESH)

    def row_coefs():
        for b in range(rb + 2):
            for k in range(5):
                for l in range(2):
                    line = crow[b + 1, k:k + 1, l * LANES:(l + 1) * LANES]
                    rc[k, (2 * b + l) * LANES:(2 * b + l + 1) * LANES, :] = jnp.transpose(
                        jnp.broadcast_to(line, (LANES, LANES)))

    def row_block(src, src_off, dst, b):
        def body(t, _):
            r0 = b * MAPX + t * TILE
            w = [rc[k, pl.ds(pl.multiple_of(MAPX + r0, 8), TILE), :] for k in range(5)]
            for l in range(V.shape[0]):
                def get(offset):
                    return src[l, pl.ds(src_off + r0 + offset, TILE), :]
                r = w[0] * get(0) + w[1] * get(-1)
                r = r + w[2] * get(1)
                r = r + w[3] * get(-MAPX) + w[4] * get(MAPX)
                dst(l, r0, r)
            return 0
        lax.fori_loop(0, MAPX // TILE, body, 0)

    def to_y(l, r0, r):
        Y[l, pl.ds(pl.multiple_of(MAPX + r0, 8), TILE), :] = r

    def to_out(l, r0, r):
        moved_ref[pl.ds(pl.multiple_of(r0, 8), TILE), l * LANES:(l + 1) * LANES] = r

    n_stage = len(bits)
    rs_copy(0).start()
    row_coefs()
    for b in range(1, rb - 1):
        row_block(V, H, to_y, b)
    for s in range(n_stage):
        rs_finish(s)
        if s + 1 < n_stage:
            rs_copy(s + 1).start()
    mine = pl.ds(pl.multiple_of(offs[n_stage], 8), n_obs >> n_stage)
    obs[mine, :] = part[mine, :]

    def halo_wait(d):
        @pl.when(has_up)
        def _():
            hcopy(d, 0).wait_send()
            hcopy(d, 1).wait_recv()

        @pl.when(has_down)
        def _():
            hcopy(d, 1).wait_send()
            hcopy(d, 0).wait_recv()

    for s in reversed(range(n_stage)):
        ag_copy(s).start()
        if s == n_stage - 1:
            for d in range(half // 2):
                halo_wait(d)
            row_block(V, H, to_y, 0)
            row_block(V, H, to_y, rb - 1)
            for b in range(1, rb - 1):
                row_block(Y, MAPX, to_out, b)
        ag_copy(s).wait()
    obs_out[...] = obs[...]
    for d in range(half // 2, half):
        halo_wait(d)
    row_block(V, H, to_y, -1)
    row_block(V, H, to_y, rb)
    row_block(Y, MAPX, to_out, 0)
    row_block(Y, MAPX, to_out, rb - 1)


def observe_block(V, ah, al, part, b, first, H, cols):
    a_hi, a_lo = ah[b], al[b]
    for j in range(cols // MAPX):
        rows = slice(H + b * MAPX, H + (b + 1) * MAPX)
        x = jnp.concatenate([V[2 * j, rows, :], V[2 * j + 1, rows, :]], axis=1)
        x_hi, x_lo = split(x)
        r = dot(a_hi, x_hi) + dot(a_hi, x_lo) + dot(a_lo, x_hi)
        at = slice(j * MAPX, (j + 1) * MAPX)
        if first:
            part[:, at] = r
        else:
            part[:, at] = part[:, at] + r


def update_kernel(moved_ref, gain_ref, obs_ref, out_ref):
    o_hi, o_lo = split(obs_ref[...])
    g = gain_ref[...]
    out_ref[...] = moved_ref[...] - (dot(g, o_hi) + dot(g, o_lo))


def local(nr, nc, covariance, wind_mask, wind_speed, obs_cells, obs_scale, gain):
    rows, cols = covariance.shape
    n_obs = obs_cells.shape[0]
    H = 2 * MAPX
    nl = cols // LANES
    rb, cb = rows // MAPX, cols // MAPX
    nchunk = rows // CHUNK
    stages = nr.bit_length() - 1
    f32, bf16 = jnp.float32, jnp.bfloat16
    vmem = pl.BlockSpec(memory_space=pltpu.VMEM)
    dma = pltpu.SemaphoreType.DMA
    moved, obs = pl.pallas_call(
        functools.partial(kernel, nr, nc),
        out_shape=(jax.ShapeDtypeStruct((rows, cols), f32), jax.ShapeDtypeStruct((n_obs, cols), f32)),
        in_specs=[pl.BlockSpec(memory_space=pl.ANY), vmem, vmem, vmem, pl.BlockSpec(memory_space=pltpu.SMEM)],
        out_specs=(vmem, vmem),
        scratch_shapes=[
            pltpu.VMEM((rows, cols), f32),
            pltpu.VMEM((rows, cols), f32),
            pltpu.VMEM((rows, cols), f32),
            pltpu.VMEM((nl, rows + 2 * H, LANES), f32),
            pltpu.VMEM((nl, rows + H, LANES), f32),
            pltpu.VMEM((cb + 4, 8, MAPX), f32),
            pltpu.VMEM((rb + 4, 8, MAPX), f32),
            pltpu.VMEM((5, rows + H, LANES), f32),
            pltpu.VMEM((n_obs * (rows + 2 * H) // LANES, LANES), f32),
            pltpu.VMEM((rb + 4, n_obs, MAPX), f32),
            pltpu.VMEM((rb + 2, n_obs, MAPX), f32),
            pltpu.VMEM((rb, n_obs, MAPX), bf16),
            pltpu.VMEM((rb, n_obs, MAPX), bf16),
            pltpu.VMEM((n_obs, cols), f32),
            pltpu.VMEM((n_obs, cols), f32),
            pltpu.VMEM((n_obs, cols), f32),
            dma(()),
            dma((2, nchunk)), dma((2, nchunk)),
            dma((2, nchunk // 2)), dma((2, nchunk // 2)),
            dma((stages,)), dma((stages,)), dma((stages,)), dma((stages,)),
        ],
        compiler_params=pltpu.CompilerParams(
            collective_id=0, has_side_effects=True, vmem_limit_bytes=48 * 1024 * 1024),
        cost_estimate=pl.CostEstimate(flops=2 * 10 ** 9, bytes_accessed=10 ** 7, transcendentals=0),
    )(covariance, wind_mask, wind_speed, obs_cells, obs_scale)
    block = MAPX
    return pl.pallas_call(
        update_kernel,
        grid=(rows // block,),
        out_shape=jax.ShapeDtypeStruct((rows, cols), f32),
        in_specs=[
            pl.BlockSpec((block, cols), lambda i: (i, 0)),
            pl.BlockSpec((block, n_obs), lambda i: (i, 0)),
            pl.BlockSpec((n_obs, cols), lambda i: (0, 0)),
        ],
        out_specs=pl.BlockSpec((block, cols), lambda i: (i, 0)),
        cost_estimate=pl.CostEstimate(flops=10 ** 9, bytes_accessed=5 * 10 ** 6, transcendentals=0),
        compiler_params=pltpu.CompilerParams(vmem_limit_bytes=24 * 1024 * 1024),
    )(moved, gain, obs)


def solution(mesh):
    placed = (P("row", "col"), P(), P(), P(), P(), P("row", None))
    return jax.shard_map(
        functools.partial(local, mesh.shape["row"], mesh.shape["col"]),
        mesh=mesh, in_specs=placed, out_specs=P("row", "col"), check_vma=False
    )
```

```python
import functools

import jax
import jax.numpy as jnp
from jax import lax
from jax.experimental import pallas as pl
from jax.experimental.pallas import tpu as pltpu
from jax.sharding import PartitionSpec as P

MAPX = 256
LANES = 128
CHUNK = 128
TILE = 16
diffusion = 0.05
MESH = pl.DeviceIdType.MESH


def split(x):
    high = x.astype(jnp.bfloat16)
    return high, (x - high.astype(jnp.float32)).astype(jnp.bfloat16)


def dot(a, b):
    return jnp.dot(a, b, preferred_element_type=jnp.float32)


def coef_block(mask_ref, speed_ref, g, map_rows):
    inside = jnp.logical_and(g >= 0, g < map_rows)
    start = pl.multiple_of(jnp.clip(g, 0, map_rows - 1) * MAPX, MAPX)
    where = pl.ds(start, MAPX)
    speed_x = speed_ref[0:1, where]
    speed_y = speed_ref[1:2, where]
    sign_x = mask_ref[0:1, where].astype(jnp.float32)
    sign_y = mask_ref[1:2, where].astype(jnp.float32)
    column = lax.broadcasted_iota(jnp.int32, (1, MAPX), 1)
    valid = jnp.where(inside, 1.0, 0.0)
    north = jnp.where(g > 0, valid, 0.0)
    south = jnp.where(g < map_rows - 1, valid, 0.0)
    return (
        (1.0 - speed_x - speed_y - 4.0 * diffusion) * valid,
        jnp.where(column > 0, speed_x * sign_x + diffusion, 0.0) * valid,
        jnp.where(column < MAPX - 1, speed_x * (1.0 - sign_x) + diffusion, 0.0) * valid,
        (speed_y * sign_y + diffusion) * north,
        (speed_y * (1.0 - sign_y) + diffusion) * south,
    )


def kernel(
    nr, nc, cov, mask_hbm, speed_hbm, cells_hbm, scale_hbm,
    moved_out, obs_out,
    moved_ref, out_sem,
    mask_ref, speed_ref, cells_ref, scale_ref, in_sem, relay_buf, rl_s, rl_r, fw_s,
    own, lh, rh, V, Y, ccol, crow, rc, sbuf, s2, tbuf, ah, al, part, rsbuf, obs,
    own_sem, zs, zr, hs, hr, rs_s, rs_r, ag_s, ag_r,
):
    rows, cols = cov.shape
    n_obs = cells_ref.shape[0]
    map_rows = speed_ref.shape[1] // MAPX
    H = 2 * MAPX
    rb, cb = rows // MAPX, cols // MAPX
    nchunk = rows // CHUNK
    half = nchunk // 2
    me_r, me_c = lax.axis_index("row"), lax.axis_index("col")
    has_up, has_down = me_r > 0, me_r < nr - 1
    has_left, has_right = me_c > 0, me_c < nc - 1
    up, down, left, right = me_r - 1, me_r + 1, me_c - 1, me_c + 1
    bits = []
    b = nr // 2
    while b:
        bits.append(b)
        b //= 2

    barrier = pltpu.get_barrier_semaphore()
    for flag, dev in ((has_up, (up, me_c)), (has_down, (down, me_c)), (has_left, (me_r, left)), (has_right, (me_r, right))):
        @pl.when(flag)
        def _(dev=dev):
            pl.semaphore_signal(barrier, inc=1, device_id=dev, device_id_type=MESH)
    partners = []
    for b in bits:
        upper = lax.rem(me_r // b, 2)
        partner = me_r + b - 2 * b * upper
        partners.append((upper, partner))
        if b > 1:
            pl.semaphore_signal(barrier, inc=1, device_id=(partner, me_c), device_id_type=MESH)
    own_copy = pltpu.make_async_copy(cov, own, own_sem)
    small = [
        pltpu.make_async_copy(src, dst, in_sem.at[i])
        for i, (src, dst) in enumerate((
            (mask_hbm, mask_ref), (speed_hbm, speed_ref), (cells_hbm, cells_ref), (scale_hbm, scale_ref)))
    ]
    for copy in small:
        copy.start()
    own_copy.start()
    peers = len(bits) - 1
    for flag in (has_up, has_down, has_left, has_right):
        peers = peers + flag.astype(jnp.int32)
    pl.semaphore_wait(barrier, peers)

    def chunk_base(d, lower):
        if lower:
            q = half // 2
            index = half + q + d - half * (d // q)
        else:
            index = d
        return pl.multiple_of(index * CHUNK, CHUNK)

    def zcopy(d, lower, side):
        base = chunk_base(d, lower)
        slot = d * 2 + lower
        dst = (rh, lh)[side]
        return pltpu.make_async_remote_copy(
            src_ref=cov.at[pl.ds(base, CHUNK), :], dst_ref=dst.at[pl.ds(base, CHUNK), :],
            send_sem=zs.at[side, slot], recv_sem=zr.at[side, slot],
            device_id=(me_r, (left, right)[side]), device_id_type=MESH)

    def hcopy(d, lower):
        base = chunk_base(d, lower)
        dst = base - H if lower else base + H + rows
        return pltpu.make_async_remote_copy(
            src_ref=V.at[:, pl.ds(H + base, CHUNK), :],
            dst_ref=V.at[:, pl.ds(pl.multiple_of(dst, CHUNK), CHUNK), :],
            send_sem=hs.at[lower, d], recv_sem=hr.at[lower, d],
            device_id=(down if lower else up, me_c), device_id_type=MESH)

    relay = nr == 4

    def far(lower):
        return me_r == (nr // 2 - 1 if lower else nr // 2)

    def corner(lower):
        return me_r == (nr - 1 if lower else 0)

    def relayed(d):
        return relay and d % 2 == 0

    def rcopy(d, lower):
        return pltpu.make_async_remote_copy(
            src_ref=V.at[:, pl.ds(H + chunk_base(d, lower), CHUNK), :], dst_ref=relay_buf.at[d // 2],
            send_sem=rl_s.at[d // 2], recv_sem=rl_r.at[d // 2],
            device_id=(me_r + nr // 2 if lower else me_r - nr // 2, me_c), device_id_type=MESH)

    def fcopy(d, lower):
        base = chunk_base(d, lower)
        dst = base - H if lower else base + H + rows
        return pltpu.make_async_remote_copy(
            src_ref=relay_buf.at[d // 2],
            dst_ref=V.at[:, pl.ds(pl.multiple_of(dst, CHUNK), CHUNK), :],
            send_sem=fw_s.at[d // 2], recv_sem=hr.at[lower, d],
            device_id=(up if lower else down, me_c), device_id_type=MESH)

    def forward(d):
        if relayed(d):
            for lower in (0, 1):
                @pl.when(corner(lower))
                def _():
                    rcopy(d, lower).wait_recv()
                    fcopy(d, lower).start()

    def hstart(d, lower):
        flag = has_down if lower else has_up
        if relayed(d):
            @pl.when(far(lower))
            def _():
                rcopy(d, lower).start()
            flag = jnp.logical_and(flag, jnp.logical_not(far(lower)))

        @pl.when(flag)
        def _():
            hcopy(d, lower).start()

    def hsent(d, lower):
        flag = has_down if lower else has_up
        if relayed(d):
            @pl.when(far(lower))
            def _():
                rcopy(d, lower).wait_send()

            @pl.when(corner(lower))
            def _():
                fcopy(d, lower).wait_send()
            flag = jnp.logical_and(flag, jnp.logical_not(far(lower)))

        @pl.when(flag)
        def _():
            hcopy(d, lower).wait_send()

    def zstart(d, _):
        for lower in (0, 1):
            @pl.when(has_left)
            def _():
                zcopy(d, lower, 0).start()

            @pl.when(has_right)
            def _():
                zcopy(d, lower, 1).start()
        return 0

    lax.fori_loop(0, half, zstart, 0)

    @pl.when(jnp.logical_not(has_left))
    def _():
        lh[...] = jnp.zeros_like(lh)

    @pl.when(jnp.logical_not(has_right))
    def _():
        rh[...] = jnp.zeros_like(rh)

    @pl.when(jnp.logical_not(has_up))
    def _():
        V[:, 0:H, :] = jnp.zeros((V.shape[0], H, LANES), jnp.float32)

    @pl.when(jnp.logical_not(has_down))
    def _():
        V[:, H + rows:, :] = jnp.zeros((V.shape[0], H, LANES), jnp.float32)

    for copy in small:
        copy.wait()
    for b in range(cb + 4):
        for k, v in enumerate(coef_block(mask_ref, speed_ref, me_c * cb + b - 2, map_rows)):
            ccol[b, k:k + 1, :] = v
    for b in range(rb + 4):
        for k, v in enumerate(coef_block(mask_ref, speed_ref, me_r * rb + b - 2, map_rows)):
            crow[b, k:k + 1, :] = v

    own_copy.wait()

    def col_step(v, first, count):
        out = []
        for i in range(count):
            c = [ccol[first + i, k:k + 1, :] for k in range(5)]
            x = v[i + 1]
            r = c[0] * x + c[1] * pltpu.roll(x, 1, 1)
            r = r + c[2] * pltpu.roll(x, MAPX - 1, 1)
            out.append(r + c[3] * v[i] + c[4] * v[i + 2])
        return out

    def col_chunk(base):
        def body(t, _):
            at = pl.ds(pl.multiple_of(base + t * TILE, TILE), TILE)
            v = [lh[at, cols - H + j * MAPX:cols - H + (j + 1) * MAPX] for j in range(2)]
            v += [own[at, j * MAPX:(j + 1) * MAPX] for j in range(cb)]
            v += [rh[at, j * MAPX:(j + 1) * MAPX] for j in range(2)]
            y = col_step(v, 1, cb + 2)
            z = col_step(y, 2, cb)
            put = pl.ds(pl.multiple_of(H + base + t * TILE, TILE), TILE)
            for j in range(cb):
                for l in range(2):
                    V[2 * j + l, put, :] = z[j][:, l * LANES:(l + 1) * LANES]
            return 0
        lax.fori_loop(0, CHUNK // TILE, body, 0)

    wide = rows + 2 * H
    nh = wide // LANES
    origin = me_r * rows - H
    lo_iota = lax.broadcasted_iota(jnp.int32, (LANES, LANES), 0)
    hi_iota = lax.broadcasted_iota(jnp.int32, (nh, LANES), 0)

    def count_group(g, _):
        base = pl.multiple_of(g * 8, 8)
        idx = cells_ref[pl.ds(base, 8), :] - origin
        hi = lax.shift_right_arithmetic(idx, 7)
        lo = jnp.bitwise_and(idx, LANES - 1)
        for i in range(8):
            one_hi = jnp.where(hi[i:i + 1, :] == hi_iota, 1.0, 0.0).astype(jnp.bfloat16)
            one_lo = jnp.where(lo[i:i + 1, :] == lo_iota, 1.0, 0.0).astype(jnp.bfloat16)
            counts = lax.dot_general(one_hi, one_lo, (((1,), (1,)), ((), ())), preferred_element_type=jnp.float32)
            sbuf[pl.ds(pl.multiple_of((base + i) * nh, 8), nh), :] = counts * scale_ref[base + i]
        return 0

    nrc = (rows + H) // LANES
    groups = n_obs // 8
    for d in range(half):
        for lower in (0, 1):
            @pl.when(has_left)
            def _():
                zcopy(d, lower, 0).wait_send()
                zcopy(d, lower, 1).wait_recv()

            @pl.when(has_right)
            def _():
                zcopy(d, lower, 1).wait_send()
                zcopy(d, lower, 0).wait_recv()
            col_chunk(chunk_base(d, lower))
            hstart(d, lower)
        if d > 0 and d < half - 1:
            forward(d - 1)
        if d < half - 1:
            g0 = groups * d // (half - 1)
            g1 = groups * (d + 1) // (half - 1)
            lax.fori_loop(g0, g1, count_group, 0)
        if d == half - 2:
            for h in range(nh):
                s2[h // 2, :, (h % 2) * LANES:(h % 2 + 1) * LANES] = sbuf[pl.ds(h, n_obs, stride=nh), :]

            def adjoint(src, at, b, offset):
                def get(i):
                    return src[i - offset, at, :]
                c = [crow[b, k:k + 1, :] for k in range(3)]
                x = get(b)
                r = c[0] * x + pltpu.roll(c[1] * x, MAPX - 1, 1) + pltpu.roll(c[2] * x, 1, 1)
                return r + crow[b + 1, 3:4, :] * get(b + 1) + crow[b - 1, 4:5, :] * get(b - 1)

            def step_one(t, _):
                at = pl.ds(pl.multiple_of(t * TILE, TILE), TILE)
                for b in range(1, rb + 3):
                    tbuf[b - 1, at, :] = adjoint(s2, at, b, 0)
                return 0

            def step_two(t, _):
                at = pl.ds(pl.multiple_of(t * TILE, TILE), TILE)
                for b in range(2, rb + 2):
                    a_hi, a_lo = split(adjoint(tbuf, at, b, 1))
                    ah[b - 2, at, :] = a_hi
                    al[b - 2, at, :] = a_lo
                return 0

            lax.fori_loop(0, n_obs // TILE, step_one, 0)
            lax.fori_loop(0, n_obs // TILE, step_two, 0)
            for b in (0, rb - 1):
                observe_block(V, ah, al, part, b, b == 0, H, cols)
    for b in range(1, rb - 1):
        observe_block(V, ah, al, part, b, False, H, cols)

    def rs_copy(s):
        upper, partner = partners[s]
        size = n_obs >> (s + 1)
        src = offs[s] + (1 - upper) * size
        return pltpu.make_async_remote_copy(
            src_ref=part.at[pl.ds(pl.multiple_of(src, 8), size), :],
            dst_ref=rsbuf.at[pl.ds(n_obs - 2 * size, size), :],
            send_sem=rs_s.at[s], recv_sem=rs_r.at[s], device_id=(partner, me_c), device_id_type=MESH)

    offs = [jnp.int32(0)]
    for s in range(len(bits)):
        offs.append(offs[s] + partners[s][0] * (n_obs >> (s + 1)))

    def rs_finish(s):
        size = n_obs >> (s + 1)
        copy = rs_copy(s)
        copy.wait()
        at = pl.ds(pl.multiple_of(offs[s + 1], 8), size)
        part[at, :] = part[at, :] + rsbuf[n_obs - 2 * size:n_obs - size, :]

    def ag_copy(s):
        size = n_obs >> (s + 1)
        at = pl.ds(pl.multiple_of(offs[s + 1], 8), size)
        return pltpu.make_async_remote_copy(
            src_ref=obs.at[at, :], dst_ref=obs.at[at, :],
            send_sem=ag_s.at[s], recv_sem=ag_r.at[s], device_id=(partners[s][1], me_c), device_id_type=MESH)

    def row_coefs():
        for b in range(rb + 2):
            for k in range(5):
                for l in range(2):
                    line = crow[b + 1, k:k + 1, l * LANES:(l + 1) * LANES]
                    rc[k, (2 * b + l) * LANES:(2 * b + l + 1) * LANES, :] = jnp.transpose(
                        jnp.broadcast_to(line, (LANES, LANES)))

    def row_block(src, src_off, dst, b):
        def body(t, _):
            r0 = b * MAPX + t * TILE
            w = [rc[k, pl.ds(pl.multiple_of(MAPX + r0, 8), TILE), :] for k in range(5)]
            for l in range(V.shape[0]):
                def get(offset):
                    return src[l, pl.ds(src_off + r0 + offset, TILE), :]
                r = w[0] * get(0) + w[1] * get(-1)
                r = r + w[2] * get(1)
                r = r + w[3] * get(-MAPX) + w[4] * get(MAPX)
                dst(l, r0, r)
            return 0
        lax.fori_loop(0, MAPX // TILE, body, 0)

    def to_y(l, r0, r):
        Y[l, pl.ds(pl.multiple_of(MAPX + r0, 8), TILE), :] = r

    def to_out(l, r0, r):
        moved_ref[pl.ds(pl.multiple_of(r0, 8), TILE), l * LANES:(l + 1) * LANES] = r

    def put(b):
        at = pl.ds(b * MAPX, MAPX)
        return pltpu.make_async_copy(moved_ref.at[at, :], moved_out.at[at, :], out_sem.at[b])

    n_stage = len(bits)
    rs_copy(0).start()
    forward(half - 2)
    row_coefs()
    for b in range(1, rb - 1):
        row_block(V, H, to_y, b)
    for s in range(n_stage):
        rs_finish(s)
        if s + 1 < n_stage:
            rs_copy(s + 1).start()
    mine = pl.ds(pl.multiple_of(offs[n_stage], 8), n_obs >> n_stage)
    obs[mine, :] = part[mine, :]

    def halo_wait(d):
        @pl.when(has_up)
        def _():
            hcopy(d, 1).wait_recv()

        @pl.when(has_down)
        def _():
            hcopy(d, 0).wait_recv()
        for lower in (0, 1):
            hsent(d, lower)

    for s in reversed(range(n_stage)):
        ag_copy(s).start()
        if s == n_stage - 1:
            for d in range(half // 2):
                halo_wait(d)
            row_block(V, H, to_y, 0)
            row_block(V, H, to_y, rb - 1)
            for b in range(1, rb - 1):
                row_block(Y, MAPX, to_out, b)
                put(b).start()
        ag_copy(s).wait()
    obs_put = pltpu.make_async_copy(obs, obs_out, out_sem.at[rb])
    obs_put.start()
    for d in range(half // 2, half):
        halo_wait(d)
    row_block(V, H, to_y, -1)
    row_block(V, H, to_y, rb)
    row_block(Y, MAPX, to_out, 0)
    put(0).start()
    row_block(Y, MAPX, to_out, rb - 1)
    put(rb - 1).start()
    obs_put.wait()
    for b in range(rb):
        put(b).wait()


def observe_block(V, ah, al, part, b, first, H, cols):
    a_hi, a_lo = ah[b], al[b]
    for j in range(cols // MAPX):
        rows = slice(H + b * MAPX, H + (b + 1) * MAPX)
        x = jnp.concatenate([V[2 * j, rows, :], V[2 * j + 1, rows, :]], axis=1)
        x_hi, x_lo = split(x)
        r = dot(a_hi, x_hi) + dot(a_hi, x_lo) + dot(a_lo, x_hi)
        at = slice(j * MAPX, (j + 1) * MAPX)
        if first:
            part[:, at] = r
        else:
            part[:, at] = part[:, at] + r


def update_kernel(moved_ref, gain_ref, obs_ref, out_ref):
    o_hi, o_lo = split(obs_ref[...])
    g = gain_ref[...]
    out_ref[...] = moved_ref[...] - (dot(g, o_hi) + dot(g, o_lo))


def local(nr, nc, covariance, wind_mask, wind_speed, obs_cells, obs_scale, gain):
    rows, cols = covariance.shape
    n_obs = obs_cells.shape[0]
    H = 2 * MAPX
    nl = cols // LANES
    rb, cb = rows // MAPX, cols // MAPX
    nchunk = rows // CHUNK
    stages = nr.bit_length() - 1
    f32, bf16 = jnp.float32, jnp.bfloat16
    dma = pltpu.SemaphoreType.DMA
    moved, obs = pl.pallas_call(
        functools.partial(kernel, nr, nc),
        out_shape=(jax.ShapeDtypeStruct((rows, cols), f32), jax.ShapeDtypeStruct((n_obs, cols), f32)),
        in_specs=[pl.BlockSpec(memory_space=pltpu.HBM)] * 5,
        out_specs=(pl.BlockSpec(memory_space=pltpu.HBM),) * 2,
        scratch_shapes=[
            pltpu.VMEM((rows, cols), f32),
            dma((rb + 1,)),
            pltpu.VMEM(wind_mask.shape, jnp.int32),
            pltpu.VMEM(wind_speed.shape, f32),
            pltpu.VMEM(obs_cells.shape, jnp.int32),
            pltpu.SMEM(obs_scale.shape, f32),
            dma((4,)),
            pltpu.VMEM((nchunk // 4, nl, CHUNK, LANES), f32),
            dma((nchunk // 4,)), dma((nchunk // 4,)), dma((nchunk // 4,)),
            pltpu.VMEM((rows, cols), f32),
            pltpu.VMEM((rows, cols), f32),
            pltpu.VMEM((rows, cols), f32),
            pltpu.VMEM((nl, rows + 2 * H, LANES), f32),
            pltpu.VMEM((nl, rows + H, LANES), f32),
            pltpu.VMEM((cb + 4, 8, MAPX), f32),
            pltpu.VMEM((rb + 4, 8, MAPX), f32),
            pltpu.VMEM((5, rows + H, LANES), f32),
            pltpu.VMEM((n_obs * (rows + 2 * H) // LANES, LANES), f32),
            pltpu.VMEM((rb + 4, n_obs, MAPX), f32),
            pltpu.VMEM((rb + 2, n_obs, MAPX), f32),
            pltpu.VMEM((rb, n_obs, MAPX), bf16),
            pltpu.VMEM((rb, n_obs, MAPX), bf16),
            pltpu.VMEM((n_obs, cols), f32),
            pltpu.VMEM((n_obs, cols), f32),
            pltpu.VMEM((n_obs, cols), f32),
            dma(()),
            dma((2, nchunk)), dma((2, nchunk)),
            dma((2, nchunk // 2)), dma((2, nchunk // 2)),
            dma((stages,)), dma((stages,)), dma((stages,)), dma((stages,)),
        ],
        compiler_params=pltpu.CompilerParams(
            collective_id=0, has_side_effects=True, vmem_limit_bytes=60 * 1024 * 1024),
        cost_estimate=pl.CostEstimate(flops=2 * 10 ** 9, bytes_accessed=10 ** 7, transcendentals=0),
    )(covariance, wind_mask, wind_speed, obs_cells, obs_scale)
    block = MAPX
    return pl.pallas_call(
        update_kernel,
        grid=(rows // block,),
        out_shape=jax.ShapeDtypeStruct((rows, cols), f32),
        in_specs=[
            pl.BlockSpec((block, cols), lambda i: (i, 0)),
            pl.BlockSpec((block, n_obs), lambda i: (i, 0)),
            pl.BlockSpec((n_obs, cols), lambda i: (0, 0)),
        ],
        out_specs=pl.BlockSpec((block, cols), lambda i: (i, 0)),
        cost_estimate=pl.CostEstimate(flops=10 ** 9, bytes_accessed=5 * 10 ** 6, transcendentals=0),
        compiler_params=pltpu.CompilerParams(vmem_limit_bytes=60 * 1024 * 1024),
    )(moved, gain, obs)


def solution(mesh):
    placed = (P("row", "col"), P(), P(), P(), P(), P("row", None))
    return jax.shard_map(
        functools.partial(local, mesh.shape["row"], mesh.shape["col"]),
        mesh=mesh, in_specs=placed, out_specs=P("row", "col"), check_vma=False
    )
```

```python
import functools

import jax
import jax.numpy as jnp
from jax import lax
from jax.experimental import pallas as pl
from jax.experimental.pallas import tpu as pltpu
from jax.sharding import PartitionSpec as P

MAPX = 256
LANES = 128
CHUNK = 128
TILE = 16
diffusion = 0.05
MESH = pl.DeviceIdType.MESH


def split(x):
    high = x.astype(jnp.bfloat16)
    return high, (x - high.astype(jnp.float32)).astype(jnp.bfloat16)


def dot(a, b):
    return jnp.dot(a, b, preferred_element_type=jnp.float32)


def coef_block(mask_ref, speed_ref, g, map_rows):
    inside = jnp.logical_and(g >= 0, g < map_rows)
    start = pl.multiple_of(jnp.clip(g, 0, map_rows - 1) * MAPX, MAPX)
    where = pl.ds(start, MAPX)
    speed_x = speed_ref[0:1, where]
    speed_y = speed_ref[1:2, where]
    sign_x = mask_ref[0:1, where].astype(jnp.float32)
    sign_y = mask_ref[1:2, where].astype(jnp.float32)
    column = lax.broadcasted_iota(jnp.int32, (1, MAPX), 1)
    valid = jnp.where(inside, 1.0, 0.0)
    north = jnp.where(g > 0, valid, 0.0)
    south = jnp.where(g < map_rows - 1, valid, 0.0)
    return (
        (1.0 - speed_x - speed_y - 4.0 * diffusion) * valid,
        jnp.where(column > 0, speed_x * sign_x + diffusion, 0.0) * valid,
        jnp.where(column < MAPX - 1, speed_x * (1.0 - sign_x) + diffusion, 0.0) * valid,
        (speed_y * sign_y + diffusion) * north,
        (speed_y * (1.0 - sign_y) + diffusion) * south,
    )


def kernel(
    nr, nc, cov, mask_hbm, speed_hbm, cells_hbm, scale_hbm, gain_hbm,
    moved_out,
    gain_ref, moved_ref, out_sem,
    mask_ref, speed_ref, cells_ref, scale_ref, in_sem, relay_buf, rl_s, rl_r, fw_s,
    own, lh, rh, V, Y, ccol, crow, rc, sbuf, s2, tbuf, ah, al, part, rsbuf, obs,
    own_sem, zs, zr, hs, hr, rs_s, rs_r, ag_s, ag_r,
):
    rows, cols = cov.shape
    n_obs = cells_ref.shape[0]
    map_rows = speed_ref.shape[1] // MAPX
    H = 2 * MAPX
    rb, cb = rows // MAPX, cols // MAPX
    nchunk = rows // CHUNK
    half = nchunk // 2
    me_r, me_c = lax.axis_index("row"), lax.axis_index("col")
    has_up, has_down = me_r > 0, me_r < nr - 1
    has_left, has_right = me_c > 0, me_c < nc - 1
    up, down, left, right = me_r - 1, me_r + 1, me_c - 1, me_c + 1
    bits = []
    b = nr // 2
    while b:
        bits.append(b)
        b //= 2

    barrier = pltpu.get_barrier_semaphore()
    for flag, dev in ((has_up, (up, me_c)), (has_down, (down, me_c)), (has_left, (me_r, left)), (has_right, (me_r, right))):
        @pl.when(flag)
        def _(dev=dev):
            pl.semaphore_signal(barrier, inc=1, device_id=dev, device_id_type=MESH)
    partners = []
    for b in bits:
        upper = lax.rem(me_r // b, 2)
        partner = me_r + b - 2 * b * upper
        partners.append((upper, partner))
        if b > 1:
            pl.semaphore_signal(barrier, inc=1, device_id=(partner, me_c), device_id_type=MESH)
    own_copy = pltpu.make_async_copy(cov, own, own_sem)
    small = [
        pltpu.make_async_copy(src, dst, in_sem.at[i])
        for i, (src, dst) in enumerate((
            (mask_hbm, mask_ref), (speed_hbm, speed_ref), (cells_hbm, cells_ref), (scale_hbm, scale_ref),
            (gain_hbm, gain_ref)))
    ]
    for copy in small:
        copy.start()
    own_copy.start()
    peers = len(bits) - 1
    for flag in (has_up, has_down, has_left, has_right):
        peers = peers + flag.astype(jnp.int32)
    pl.semaphore_wait(barrier, peers)

    def chunk_base(d, lower):
        if lower:
            q = half // 2
            index = half + q + d - half * (d // q)
        else:
            index = d
        return pl.multiple_of(index * CHUNK, CHUNK)

    def zcopy(d, lower, side):
        base = chunk_base(d, lower)
        slot = d * 2 + lower
        dst = (rh, lh)[side]
        return pltpu.make_async_remote_copy(
            src_ref=cov.at[pl.ds(base, CHUNK), :], dst_ref=dst.at[pl.ds(base, CHUNK), :],
            send_sem=zs.at[side, slot], recv_sem=zr.at[side, slot],
            device_id=(me_r, (left, right)[side]), device_id_type=MESH)

    def hcopy(d, lower):
        base = chunk_base(d, lower)
        dst = base - H if lower else base + H + rows
        return pltpu.make_async_remote_copy(
            src_ref=V.at[:, pl.ds(H + base, CHUNK), :],
            dst_ref=V.at[:, pl.ds(pl.multiple_of(dst, CHUNK), CHUNK), :],
            send_sem=hs.at[lower, d], recv_sem=hr.at[lower, d],
            device_id=(down if lower else up, me_c), device_id_type=MESH)

    relay = nr == 4

    def far(lower):
        return me_r == (nr // 2 - 1 if lower else nr // 2)

    def corner(lower):
        return me_r == (nr - 1 if lower else 0)

    def relayed(d):
        return relay and d % 2 == 0

    def rcopy(d, lower):
        return pltpu.make_async_remote_copy(
            src_ref=V.at[:, pl.ds(H + chunk_base(d, lower), CHUNK), :], dst_ref=relay_buf.at[d // 2],
            send_sem=rl_s.at[d // 2], recv_sem=rl_r.at[d // 2],
            device_id=(me_r + nr // 2 if lower else me_r - nr // 2, me_c), device_id_type=MESH)

    def fcopy(d, lower):
        base = chunk_base(d, lower)
        dst = base - H if lower else base + H + rows
        return pltpu.make_async_remote_copy(
            src_ref=relay_buf.at[d // 2],
            dst_ref=V.at[:, pl.ds(pl.multiple_of(dst, CHUNK), CHUNK), :],
            send_sem=fw_s.at[d // 2], recv_sem=hr.at[lower, d],
            device_id=(up if lower else down, me_c), device_id_type=MESH)

    def forward(d):
        if relayed(d):
            for lower in (0, 1):
                @pl.when(corner(lower))
                def _():
                    rcopy(d, lower).wait_recv()
                    fcopy(d, lower).start()

    def hstart(d, lower):
        flag = has_down if lower else has_up
        if relayed(d):
            @pl.when(far(lower))
            def _():
                rcopy(d, lower).start()
            flag = jnp.logical_and(flag, jnp.logical_not(far(lower)))

        @pl.when(flag)
        def _():
            hcopy(d, lower).start()

    def hsent(d, lower):
        flag = has_down if lower else has_up
        if relayed(d):
            @pl.when(far(lower))
            def _():
                rcopy(d, lower).wait_send()

            @pl.when(corner(lower))
            def _():
                fcopy(d, lower).wait_send()
            flag = jnp.logical_and(flag, jnp.logical_not(far(lower)))

        @pl.when(flag)
        def _():
            hcopy(d, lower).wait_send()

    def zstart(d, lowers=(0, 1)):
        for lower in lowers:
            @pl.when(has_left)
            def _():
                zcopy(d, lower, 0).start()

            @pl.when(has_right)
            def _():
                zcopy(d, lower, 1).start()

    zstart(0)

    @pl.when(jnp.logical_not(has_left))
    def _():
        lh[...] = jnp.zeros_like(lh)

    @pl.when(jnp.logical_not(has_right))
    def _():
        rh[...] = jnp.zeros_like(rh)

    @pl.when(jnp.logical_not(has_up))
    def _():
        V[:, 0:H, :] = jnp.zeros((V.shape[0], H, LANES), jnp.float32)

    @pl.when(jnp.logical_not(has_down))
    def _():
        V[:, H + rows:, :] = jnp.zeros((V.shape[0], H, LANES), jnp.float32)

    for copy in small:
        copy.wait()
    for b in range(cb + 4):
        for k, v in enumerate(coef_block(mask_ref, speed_ref, me_c * cb + b - 2, map_rows)):
            ccol[b, k:k + 1, :] = v
    for b in range(rb + 4):
        for k, v in enumerate(coef_block(mask_ref, speed_ref, me_r * rb + b - 2, map_rows)):
            crow[b, k:k + 1, :] = v

    own_copy.wait()

    def col_step(v, first, count):
        out = []
        for i in range(count):
            c = [ccol[first + i, k:k + 1, :] for k in range(5)]
            x = v[i + 1]
            r = c[0] * x + c[1] * pltpu.roll(x, 1, 1)
            r = r + c[2] * pltpu.roll(x, MAPX - 1, 1)
            out.append(r + c[3] * v[i] + c[4] * v[i + 2])
        return out

    def col_chunk(base):
        def body(t, _):
            at = pl.ds(pl.multiple_of(base + t * TILE, TILE), TILE)
            v = [lh[at, cols - H + j * MAPX:cols - H + (j + 1) * MAPX] for j in range(2)]
            v += [own[at, j * MAPX:(j + 1) * MAPX] for j in range(cb)]
            v += [rh[at, j * MAPX:(j + 1) * MAPX] for j in range(2)]
            y = col_step(v, 1, cb + 2)
            z = col_step(y, 2, cb)
            put = pl.ds(pl.multiple_of(H + base + t * TILE, TILE), TILE)
            for j in range(cb):
                for l in range(2):
                    V[2 * j + l, put, :] = z[j][:, l * LANES:(l + 1) * LANES]
            return 0
        lax.fori_loop(0, CHUNK // TILE, body, 0)

    wide = rows + 2 * H
    nh = wide // LANES
    origin = me_r * rows - H
    lo_iota = lax.broadcasted_iota(jnp.int32, (LANES, LANES), 0)
    hi_iota = lax.broadcasted_iota(jnp.int32, (nh, LANES), 0)

    def count_group(g, _):
        base = pl.multiple_of(g * 8, 8)
        idx = cells_ref[pl.ds(base, 8), :] - origin
        hi = lax.shift_right_arithmetic(idx, 7)
        lo = jnp.bitwise_and(idx, LANES - 1)
        for i in range(8):
            one_hi = jnp.where(hi[i:i + 1, :] == hi_iota, 1.0, 0.0).astype(jnp.bfloat16)
            one_lo = jnp.where(lo[i:i + 1, :] == lo_iota, 1.0, 0.0).astype(jnp.bfloat16)
            counts = lax.dot_general(one_hi, one_lo, (((1,), (1,)), ((), ())), preferred_element_type=jnp.float32)
            sbuf[pl.ds(pl.multiple_of((base + i) * nh, 8), nh), :] = counts * scale_ref[base + i]
        return 0

    nrc = (rows + H) // LANES
    groups = n_obs // 8
    for d in range(half):
        for lower in (0, 1):
            @pl.when(has_left)
            def _():
                zcopy(d, lower, 0).wait_send()

            @pl.when(has_right)
            def _():
                zcopy(d, lower, 1).wait_send()
            if d + 1 < half:
                zstart(d + 1, (lower,))

            @pl.when(has_left)
            def _():
                zcopy(d, lower, 1).wait_recv()

            @pl.when(has_right)
            def _():
                zcopy(d, lower, 0).wait_recv()
            col_chunk(chunk_base(d, lower))
            hstart(d, lower)
        if d > 0 and d < half - 1:
            forward(d - 1)
        if d < half - 1:
            g0 = groups * d // (half - 1)
            g1 = groups * (d + 1) // (half - 1)
            lax.fori_loop(g0, g1, count_group, 0)
        if d == half - 2:
            for h in range(nh):
                s2[h // 2, :, (h % 2) * LANES:(h % 2 + 1) * LANES] = sbuf[pl.ds(h, n_obs, stride=nh), :]

            def adjoint(src, at, b, offset):
                def get(i):
                    return src[i - offset, at, :]
                c = [crow[b, k:k + 1, :] for k in range(3)]
                x = get(b)
                r = c[0] * x + pltpu.roll(c[1] * x, MAPX - 1, 1) + pltpu.roll(c[2] * x, 1, 1)
                return r + crow[b + 1, 3:4, :] * get(b + 1) + crow[b - 1, 4:5, :] * get(b - 1)

            def step_one(t, _):
                at = pl.ds(pl.multiple_of(t * TILE, TILE), TILE)
                for b in range(1, rb + 3):
                    tbuf[b - 1, at, :] = adjoint(s2, at, b, 0)
                return 0

            def step_two(t, _):
                at = pl.ds(pl.multiple_of(t * TILE, TILE), TILE)
                for b in range(2, rb + 2):
                    a_hi, a_lo = split(adjoint(tbuf, at, b, 1))
                    ah[b - 2, at, :] = a_hi
                    al[b - 2, at, :] = a_lo
                return 0

            lax.fori_loop(0, n_obs // TILE, step_one, 0)
            lax.fori_loop(0, n_obs // TILE, step_two, 0)
            for b in (0, rb - 1):
                observe_block(V, ah, al, part, b, b == 0, H, cols)
    for b in range(1, rb - 1):
        observe_block(V, ah, al, part, b, False, H, cols)

    def rs_copy(s):
        upper, partner = partners[s]
        size = n_obs >> (s + 1)
        src = offs[s] + (1 - upper) * size
        return pltpu.make_async_remote_copy(
            src_ref=part.at[pl.ds(pl.multiple_of(src, 8), size), :],
            dst_ref=rsbuf.at[pl.ds(n_obs - 2 * size, size), :],
            send_sem=rs_s.at[s], recv_sem=rs_r.at[s], device_id=(partner, me_c), device_id_type=MESH)

    offs = [jnp.int32(0)]
    for s in range(len(bits)):
        offs.append(offs[s] + partners[s][0] * (n_obs >> (s + 1)))

    def rs_finish(s):
        size = n_obs >> (s + 1)
        copy = rs_copy(s)
        copy.wait()
        at = pl.ds(pl.multiple_of(offs[s + 1], 8), size)
        part[at, :] = part[at, :] + rsbuf[n_obs - 2 * size:n_obs - size, :]

    def ag_copy(s):
        size = n_obs >> (s + 1)
        at = pl.ds(pl.multiple_of(offs[s + 1], 8), size)
        return pltpu.make_async_remote_copy(
            src_ref=obs.at[at, :], dst_ref=obs.at[at, :],
            send_sem=ag_s.at[s], recv_sem=ag_r.at[s], device_id=(partners[s][1], me_c), device_id_type=MESH)

    def row_coefs():
        for b in range(rb + 2):
            for k in range(5):
                for l in range(2):
                    line = crow[b + 1, k:k + 1, l * LANES:(l + 1) * LANES]
                    rc[k, (2 * b + l) * LANES:(2 * b + l + 1) * LANES, :] = jnp.transpose(
                        jnp.broadcast_to(line, (LANES, LANES)))

    def row_block(src, src_off, dst, b):
        def body(t, _):
            r0 = b * MAPX + t * TILE
            w = [rc[k, pl.ds(pl.multiple_of(MAPX + r0, 8), TILE), :] for k in range(5)]
            for l in range(V.shape[0]):
                def get(offset):
                    return src[l, pl.ds(src_off + r0 + offset, TILE), :]
                r = w[0] * get(0) + w[1] * get(-1)
                r = r + w[2] * get(1)
                r = r + w[3] * get(-MAPX) + w[4] * get(MAPX)
                dst(l, r0, r)
            return 0
        lax.fori_loop(0, MAPX // TILE, body, 0)

    def to_y(l, r0, r):
        Y[l, pl.ds(pl.multiple_of(MAPX + r0, 8), TILE), :] = r

    def to_out(l, r0, r):
        moved_ref[pl.ds(pl.multiple_of(r0, 8), TILE), l * LANES:(l + 1) * LANES] = r

    def to_final(l, r0, r):
        at = pl.ds(pl.multiple_of(r0, 8), TILE)
        where = slice(l * LANES, (l + 1) * LANES)
        moved_ref[at, where] = r - moved_ref[at, where]

    def put(b):
        at = pl.ds(b * MAPX, MAPX)
        return pltpu.make_async_copy(moved_ref.at[at, :], moved_out.at[at, :], out_sem.at[b])

    n_stage = len(bits)
    rs_copy(0).start()
    forward(half - 2)
    row_coefs()
    for b in range(1, rb - 1):
        row_block(V, H, to_y, b)
    for s in range(n_stage):
        rs_finish(s)
        if s + 1 < n_stage:
            rs_copy(s + 1).start()
    mine = pl.ds(pl.multiple_of(offs[n_stage], 8), n_obs >> n_stage)
    obs[mine, :] = part[mine, :]

    def halo_wait(d):
        @pl.when(has_up)
        def _():
            hcopy(d, 1).wait_recv()

        @pl.when(has_down)
        def _():
            hcopy(d, 0).wait_recv()
        for lower in (0, 1):
            hsent(d, lower)

    for s in reversed(range(n_stage)):
        ag_copy(s).start()
        if s == n_stage - 1:
            for d in range(half // 2):
                halo_wait(d)
            row_block(V, H, to_y, 0)
            row_block(V, H, to_y, rb - 1)
            for b in range(1, rb - 1):
                row_block(Y, MAPX, to_out, b)
        ag_copy(s).wait()
    o_hi, o_lo = split(obs[...])
    for b in range(rb):
        at = slice(b * MAPX, (b + 1) * MAPX)
        update = dot(gain_ref[at, :], o_hi) + dot(gain_ref[at, :], o_lo)
        if 0 < b < rb - 1:
            moved_ref[at, :] = moved_ref[at, :] - update
            put(b).start()
        else:
            moved_ref[at, :] = update
    for d in range(half // 2, half):
        halo_wait(d)
    row_block(V, H, to_y, -1)
    row_block(V, H, to_y, rb)
    row_block(Y, MAPX, to_final, 0)
    put(0).start()
    row_block(Y, MAPX, to_final, rb - 1)
    put(rb - 1).start()
    for b in range(rb):
        put(b).wait()


def observe_block(V, ah, al, part, b, first, H, cols):
    a_hi, a_lo = ah[b], al[b]
    for j in range(cols // MAPX):
        rows = slice(H + b * MAPX, H + (b + 1) * MAPX)
        x = jnp.concatenate([V[2 * j, rows, :], V[2 * j + 1, rows, :]], axis=1)
        x_hi, x_lo = split(x)
        r = dot(a_hi, x_hi) + dot(a_hi, x_lo) + dot(a_lo, x_hi)
        at = slice(j * MAPX, (j + 1) * MAPX)
        if first:
            part[:, at] = r
        else:
            part[:, at] = part[:, at] + r


def local(nr, nc, covariance, wind_mask, wind_speed, obs_cells, obs_scale, gain):
    rows, cols = covariance.shape
    n_obs = obs_cells.shape[0]
    H = 2 * MAPX
    nl = cols // LANES
    rb, cb = rows // MAPX, cols // MAPX
    nchunk = rows // CHUNK
    stages = nr.bit_length() - 1
    f32, bf16 = jnp.float32, jnp.bfloat16
    dma = pltpu.SemaphoreType.DMA
    return pl.pallas_call(
        functools.partial(kernel, nr, nc),
        out_shape=jax.ShapeDtypeStruct((rows, cols), f32),
        in_specs=[pl.BlockSpec(memory_space=pltpu.HBM)] * 6,
        out_specs=pl.BlockSpec(memory_space=pltpu.HBM),
        scratch_shapes=[
            pltpu.VMEM(gain.shape, bf16),
            pltpu.VMEM((rows, cols), f32),
            dma((rb,)),
            pltpu.VMEM(wind_mask.shape, jnp.int32),
            pltpu.VMEM(wind_speed.shape, f32),
            pltpu.VMEM(obs_cells.shape, jnp.int32),
            pltpu.SMEM(obs_scale.shape, f32),
            dma((5,)),
            pltpu.VMEM((nchunk // 4, nl, CHUNK, LANES), f32),
            dma((nchunk // 4,)), dma((nchunk // 4,)), dma((nchunk // 4,)),
            pltpu.VMEM((rows, cols), f32),
            pltpu.VMEM((rows, cols), f32),
            pltpu.VMEM((rows, cols), f32),
            pltpu.VMEM((nl, rows + 2 * H, LANES), f32),
            pltpu.VMEM((nl, rows + H, LANES), f32),
            pltpu.VMEM((cb + 4, 8, MAPX), f32),
            pltpu.VMEM((rb + 4, 8, MAPX), f32),
            pltpu.VMEM((5, rows + H, LANES), f32),
            pltpu.VMEM((n_obs * (rows + 2 * H) // LANES, LANES), f32),
            pltpu.VMEM((rb + 4, n_obs, MAPX), f32),
            pltpu.VMEM((rb + 2, n_obs, MAPX), f32),
            pltpu.VMEM((rb, n_obs, MAPX), bf16),
            pltpu.VMEM((rb, n_obs, MAPX), bf16),
            pltpu.VMEM((n_obs, cols), f32),
            pltpu.VMEM((n_obs, cols), f32),
            pltpu.VMEM((n_obs, cols), f32),
            dma(()),
            dma((2, nchunk)), dma((2, nchunk)),
            dma((2, nchunk // 2)), dma((2, nchunk // 2)),
            dma((stages,)), dma((stages,)), dma((stages,)), dma((stages,)),
        ],
        compiler_params=pltpu.CompilerParams(
            collective_id=0, has_side_effects=True, vmem_limit_bytes=60 * 1024 * 1024),
        cost_estimate=pl.CostEstimate(flops=2 * 10 ** 9, bytes_accessed=10 ** 7, transcendentals=0),
    )(covariance, wind_mask, wind_speed, obs_cells, obs_scale, gain)


def solution(mesh):
    placed = (P("row", "col"), P(), P(), P(), P(), P("row", None))
    return jax.shard_map(
        functools.partial(local, mesh.shape["row"], mesh.shape["col"]),
        mesh=mesh, in_specs=placed, out_specs=P("row", "col"), check_vma=False
    )
```
